32 devices in a mesh: rows: 4 (over z), cols: 4 (over x, core), layers: 2 (over y).
Axes of the slice: x: 2, y: 2, z: 4, core: 2. Of those that a mesh axis runs over, the one named last changes fastest.
Arguments:
- term_now: bfloat16 [96, 128, 2048], P('rows', 'layers', 'cols'), may hold values from -6 to 6
- term_prev: bfloat16 [96, 128, 2048], P('rows', 'layers', 'cols'), may hold values from -6 to 6
- cotangent: bfloat16 [96, 128, 2048], P('rows', None, 'cols'), may hold values from -6 to 6
- ham_blocks: bfloat16 [96, 25, 128, 128], P('rows', None, 'layers'), as said below
- block_mask: int32 [96, 25], P('rows'), may hold values from 0 to 1, as said below
- ham_slope: bfloat16 [96, 25, 128, 128], P('rows', None, 'layers'), may hold values from -0.0012207031 to 0.0012207031
- atom_owner: int32 [96, 128], P('rows'), may hold values from 0 to 63, never falling along the last dimension, each value on 1 to 4 neighbouring positions
Outputs:
- term_next: bfloat16 [96, 128, 2048], P('rows', 'layers', 'cols')
- grad_term: bfloat16 [96, 128, 2048], P('rows', 'layers', 'cols')
- forces: float32 [96, 64], P('rows')
The draws below stay inside these ranges and needn't reach their ends.
Inputs may be any that keep to these rules, and one draw needn't show every extreme that they name: ham_blocks[i, d] is the transpose of ham_blocks[(i + d - 12) mod 96, 24 - d]: H is symmetric. block_mask[i, d] equals block_mask[(i + d - 12) mod 96, 24 - d], and block_mask[i, 12] is 1. Each row of atom_owner never falls; each atom owns 1 to 4 consecutive row orbitals.
All inputs are finite; a program needn't handle non-finite values.
Results may differ from the reference program's by a relative error of at most 0.005.
Values may be sent and summed in bfloat16 or wider, within the bound.
No kernel may reach another device: no remote copies, remote signals or barrier semaphores. Data moves between devices by JAX's collectives and lax.ppermute only.
A program may use at most 128 MiB of HBM per device.

```python
import math
import jax
import jax.numpy as jnp
import numpy as np
from jax import lax

B = 128
R = 12
SLOTS = 25
NB = 96
NCOL = 2048
APB = 64
N_LAYERS = 2


def draw_ham_blocks(key, part):
    full_shape = (NB, SLOTS, B, B)
    noise = jax.random.normal(key, full_shape, jnp.float32)
    row_ids = jnp.arange(NB)[:, None]
    slot_ids = jnp.arange(SLOTS)[None, :]
    partner = (row_ids + slot_ids - R) % NB
    mirror = noise[partner, SLOTS - 1 - slot_ids]
    symmetric = (noise + jnp.swapaxes(mirror, 2, 3)) * (0.5 / math.sqrt(2.0 * SLOTS * B))
    return symmetric.astype(jnp.bfloat16)


def draw_block_mask(key, part):
    raw_draw = jax.random.randint(key, (NB, SLOTS), 0, 100)
    slot_ids = jnp.arange(SLOTS)[None, :]
    row_ids = jnp.arange(NB)[:, None]
    distance = jnp.abs(slot_ids - R)
    kept = (raw_draw < 100 - 50 * distance // R).astype(jnp.int32)
    partner = (row_ids + slot_ids - R) % NB
    mirrored = kept[partner, SLOTS - 1 - slot_ids]
    return jnp.where(slot_ids >= R, kept, mirrored).astype(jnp.int32)


def levels(stream_key, shape, cuts, low, largest):
    def one(axis_at, blocks):
        draws = jax.random.uniform(jax.random.fold_in(jax.random.fold_in(stream_key, 6), axis_at), (blocks,), jnp.float32, low / len(cuts), largest / len(cuts))
        return jnp.repeat(jnp.exp(draws), shape[axis_at] // blocks).reshape((-1,) + (1,) * (len(shape) - axis_at - 1))

    level = one(*cuts[0])
    for cut in cuts[1:]:
        level = level * one(*cut)
    return level


def split_up(count, total, reach, lean):
    weights = [(1 << 20) // math.isqrt(standing ** lean) + 1 for standing in range(2, count + 1)]
    rest, holding = total - reach - (count - 1), [1] * (count - 1)
    while rest > 0:
        movable = [i for i in range(count - 1) if holding[i] < reach]
        pool, remaining = sum([weights[i] for i in movable]), rest
        for i in movable:
            more = min(reach - holding[i], max(1, remaining * weights[i] // pool), rest)
            holding[i] = holding[i] + more
            rest = rest - more
    return np.array([reach] + holding)


def uneven(rng, count, total, limit, slope):
    if count == 2:
        one = jax.random.randint(rng, (), max(1, total - limit), min(limit, total - 1) + 1)
        return jnp.stack([one, total - one])
    lengths = jnp.asarray(split_up(count, total, limit, slope), jnp.int32)
    couples = (count - 1) // 2
    source_of, sink = lengths[1:1 + 2 * couples:2], lengths[2:2 + 2 * couples:2]
    slack = jnp.minimum(source_of - 1, limit - sink)
    moved = jax.random.randint(jax.random.fold_in(rng, 1), (couples,), 0, 1 << 20) % (slack + 1)
    lengths = lengths.at[1:1 + 2 * couples:2].set(source_of - moved).at[2:2 + 2 * couples:2].set(sink + moved)
    return lengths[jax.random.permutation(jax.random.fold_in(rng, 2), count)]


def centred(stream_key, dims, width, limit, cuts=(), held_as=jnp.bfloat16):
    factor_of = levels(stream_key, dims, cuts, -0.22, 0.18) if cuts else 1.0
    result = jax.random.normal(stream_key, dims, jnp.float32) * width * factor_of
    return jnp.minimum(jnp.maximum(result, -limit), limit).astype(held_as)


def setup_inputs(seed: int = 0) -> dict:
    splits = jax.random.split(jax.random.key(seed), 8)
    return {
        "term_now": centred(splits[0], (NB, B, NCOL), 1.0, 6.0, ((0, 4), (1, 2), (2, 4))),
        "term_prev": centred(splits[1], (NB, B, NCOL), 1.0, 6.0, ((0, 4), (1, 2), (2, 4))),
        "cotangent": centred(splits[2], (NB, B, NCOL), 1.0, 6.0, ((0, 4), (2, 4))),
        "ham_blocks": draw_ham_blocks(jax.random.fold_in(splits[7], 71), 0),
        "block_mask": draw_block_mask(jax.random.fold_in(splits[7], 71), 0),
        "ham_slope": centred(splits[5], (NB, SLOTS, B, B), (4 * SLOTS * B * NCOL) ** -0.5, 0.0012207031, ((0, 4), (2, 2))),
        "atom_owner": jax.vmap(lambda own: jnp.searchsorted(jnp.cumsum(uneven(own, APB, B, 4, 0)), jnp.arange(B), side="right"))(jax.random.split(splits[6], NB)).reshape((NB, B)).astype(jnp.int32),
    }


def reference(term_now, term_prev, cotangent, ham_blocks, block_mask, ham_slope, atom_owner):
    half_rows = B // N_LAYERS
    state = term_now.astype(jnp.float32)
    cot_float = cotangent.astype(jnp.float32)
    mask_float = block_mask.astype(jnp.float32)

    def advance(offset, sums):
        forward, backward, row_force = sums
        kept = lax.dynamic_index_in_dim(mask_float, offset, 1, keepdims=False)
        masked = lax.dynamic_index_in_dim(ham_blocks, offset, 1, keepdims=False).astype(jnp.float32)
        masked = masked * kept[:, None, None]
        nearby = jnp.roll(state, R - offset, axis=0)
        split_blocks = masked.reshape(NB, N_LAYERS, half_rows, B)
        split_state = nearby.reshape(NB, N_LAYERS, half_rows, NCOL)
        forward = forward + jnp.einsum("ihnm,ihnc->himc", split_blocks, split_state)
        split_cols = masked.reshape(NB, B, N_LAYERS, half_rows)
        split_cot = cot_float.reshape(NB, N_LAYERS, half_rows, NCOL)
        sources = jnp.einsum("inhm,ihmc->hinc", split_cols, split_cot)
        backward = backward + jnp.roll(sources, offset - R, axis=1)
        pair_grads = 2.0 * kept[:, None, None] * jnp.einsum("inc,imc->inm", nearby, cot_float)
        slope_block = lax.dynamic_index_in_dim(ham_slope, offset, 1, keepdims=False).astype(jnp.float32)
        row_force = row_force + jnp.sum(pair_grads * slope_block, axis=1)
        return forward, backward, row_force

    zeros_terms = jnp.zeros((N_LAYERS, NB, B, NCOL), jnp.float32)
    initial = (zeros_terms, zeros_terms, jnp.zeros((NB, B), jnp.float32))
    forward, backward, row_force = lax.fori_loop(0, SLOTS, advance, initial)
    forward_sum = jnp.sum(forward, axis=0)
    backward_sum = jnp.sum(backward, axis=0)
    term_next = (2.0 * forward_sum - term_prev.astype(jnp.float32)).astype(jnp.bfloat16)
    grad_term = (2.0 * backward_sum).astype(jnp.bfloat16)
    atom_ids = jnp.arange(APB, dtype=jnp.int32)
    owners = (atom_owner[:, :, None] == atom_ids[None, None, :]).astype(jnp.float32)
    forces = jnp.einsum("im,ima->ia", row_force, owners)
    return term_next, grad_term, forces
```

```python
import functools

import jax
import jax.numpy as jnp
from jax import lax
from jax.experimental import pallas as pl
from jax.experimental.pallas import tpu as pltpu
from jax.sharding import PartitionSpec as P

APB = 64
VMEM_BYTES = 56 * 1024 * 1024
ARBITRARY = pltpu.GridDimensionSemantics.ARBITRARY


def shifted(value, axis, steps):
    count = lax.axis_size(axis)
    pairs = [(source, (source + steps) % count) for source in range(count)]
    return lax.ppermute(value, axis, pairs)


def swapped(value, axis, bit):
    count = lax.axis_size(axis)
    return lax.ppermute(value, axis, [(source, source ^ bit) for source in range(count)])


def keep_blocks(mask_ref, row, blocks, slots, share):
    parts = []
    for slot in range(slots):
        kept = mask_ref[row, slot] != 0
        block = blocks[slot * share : (slot + 1) * share]
        parts.append(jnp.where(kept, block, jnp.zeros_like(block)))
    return parts


def push_kernel(group, slots, share, mask_ref, ham_ref, cot_ref, low_ref, own_ref, high_ref, left, total):
    step = pl.program_id(0)
    orbitals = ham_ref.shape[2]
    columns = cot_ref.shape[2]
    spread = (slots + group - 1) * share

    @pl.when(step == 0)
    def _():
        total[...] = jnp.zeros_like(total)
        left[...] = jnp.zeros_like(left)

    for k in range(group):
        parts = keep_blocks(mask_ref, step * group + k, ham_ref[k], slots, share)
        for slot in range(slots):
            at = (slot + k) * share
            left[at : at + share, k * orbitals : (k + 1) * orbitals] = parts[slot]
    right = cot_ref[...].reshape(group * orbitals, columns)
    first = pl.multiple_of(step * (group * share), group * share)
    piece = 2 * share
    for at in range(0, spread, piece):
        size = min(piece, spread - at)
        total[pl.ds(first + at, size), :] += jnp.dot(
            left[at : at + size, :], right, preferred_element_type=jnp.float32
        )

    @pl.when(step == pl.num_programs(0) - 1)
    def _():
        halo = low_ref.shape[0]
        own = own_ref.shape[0]
        low_ref[...] = (2.0 * total[:halo, :]).astype(low_ref.dtype)
        own_ref[...] = 2.0 * total[halo : halo + own, :]
        high_ref[...] = (2.0 * total[halo + own :, :]).astype(high_ref.dtype)


def push(ham, mask, cotangent, share):
    rows, depth, orbitals = ham.shape
    columns = cotangent.shape[2]
    slots = depth // share
    reach = (slots - 1) // 2
    group = 2 if rows % 2 == 0 else 1
    kernel = functools.partial(push_kernel, group, slots, share)
    flops = 2 * rows * depth * orbitals * columns
    return pl.pallas_call(
        kernel,
        out_shape=(
            jax.ShapeDtypeStruct((reach * share, columns), jnp.bfloat16),
            jax.ShapeDtypeStruct((rows * share, columns), jnp.float32),
            jax.ShapeDtypeStruct((reach * share, columns), jnp.bfloat16),
        ),
        grid_spec=pltpu.PrefetchScalarGridSpec(
            num_scalar_prefetch=1,
            grid=(rows // group,),
            in_specs=[
                pl.BlockSpec((group, depth, orbitals), lambda i, m: (i, 0, 0)),
                pl.BlockSpec((group, orbitals, columns), lambda i, m: (i, 0, 0)),
            ],
            out_specs=[
                pl.BlockSpec((reach * share, columns), lambda i, m: (0, 0)),
                pl.BlockSpec((rows * share, columns), lambda i, m: (0, 0)),
                pl.BlockSpec((reach * share, columns), lambda i, m: (0, 0)),
            ],
            scratch_shapes=[
                pltpu.VMEM(((slots + group - 1) * share, group * orbitals), jnp.bfloat16),
                pltpu.VMEM(((rows + 2 * reach) * share, columns), jnp.float32),
            ],
        ),
        compiler_params=pltpu.CompilerParams(
            dimension_semantics=(ARBITRARY,), vmem_limit_bytes=VMEM_BYTES
        ),
        cost_estimate=pl.CostEstimate(flops=flops, bytes_accessed=ham.size * 2, transcendentals=0),
        name="push_blocks",
    )(mask, ham, cotangent)


def pull_kernel(
    first_row, slots, share, mask_ref, side_ref, ham_ref, slope_ref, cot_ref, prev_ref, head_ref, tail_ref,
    keep_ref, send_ref, force_ref, window, both, product,
):
    step = pl.program_id(0)
    orbitals = ham_ref.shape[1]
    side = side_ref[0]

    @pl.when(step == 0)
    def _():
        split = head_ref.shape[0]
        window[:split, :] = head_ref[...]
        window[split:, :] = tail_ref[...]

    row = first_row + step
    for slot in range(slots):
        kept = mask_ref[row, slot] != 0
        span = slice(slot * share, (slot + 1) * share)
        block = ham_ref[span, :]
        both[span, :orbitals] = jnp.where(kept, block, jnp.zeros_like(block))
        block = slope_ref[span, :]
        both[span, orbitals:] = jnp.where(kept, block, jnp.zeros_like(block))
    near = window[pl.ds(pl.multiple_of(step * share, share), slots * share), :]
    product[...] = lax.dot_general(
        both[...], near, (((0,), (0,)), ((), ())), preferred_element_type=jnp.float32
    )
    mine = pl.multiple_of(side * share, share)
    other = pl.multiple_of((1 - side) * share, share)
    keep_ref[...] = 2.0 * product[pl.ds(mine, share), :] - prev_ref[...].astype(jnp.float32)
    send_ref[...] = (2.0 * product[pl.ds(other, share), :]).astype(send_ref.dtype)
    work = product[orbitals:, :] * cot_ref[...].astype(jnp.float32)
    lanes = 128
    folded = work[:, :lanes]
    for at in range(lanes, work.shape[1], lanes):
        folded = folded + work[:, at : at + lanes]
    force_ref[...] = 2.0 * jnp.sum(folded.T, axis=0, keepdims=True)


def pull(ham, slope, mask, side, cotangent, previous, head, tail, share, first_row, rows):
    _, depth, orbitals = ham.shape
    columns = cotangent.shape[2]
    slots = depth // share
    kernel = functools.partial(pull_kernel, first_row, slots, share)
    flops = 4 * rows * depth * orbitals * columns
    row_block = lambda *dims: pl.BlockSpec((None,) + dims, lambda i, m, s: (i + first_row, 0, 0))
    whole = lambda a: pl.BlockSpec(a.shape, lambda i, m, s: (0, 0))
    out_block = lambda *dims: pl.BlockSpec((None,) + dims, lambda i, m, s: (i, 0, 0))
    return pl.pallas_call(
        kernel,
        out_shape=(
            jax.ShapeDtypeStruct((rows, share, columns), jnp.float32),
            jax.ShapeDtypeStruct((rows, share, columns), jnp.bfloat16),
            jax.ShapeDtypeStruct((rows, 1, orbitals), jnp.float32),
        ),
        grid_spec=pltpu.PrefetchScalarGridSpec(
            num_scalar_prefetch=2,
            grid=(rows,),
            in_specs=[
                row_block(depth, orbitals),
                row_block(depth, orbitals),
                row_block(orbitals, columns),
                row_block(share, columns),
                whole(head),
                whole(tail),
            ],
            out_specs=[
                out_block(share, columns),
                out_block(share, columns),
                out_block(1, orbitals),
            ],
            scratch_shapes=[
                pltpu.VMEM((head.shape[0] + tail.shape[0], columns), jnp.bfloat16),
                pltpu.VMEM((depth, 2 * orbitals), jnp.bfloat16),
                pltpu.VMEM((2 * orbitals, columns), jnp.float32),
            ],
        ),
        compiler_params=pltpu.CompilerParams(
            dimension_semantics=(ARBITRARY,), vmem_limit_bytes=VMEM_BYTES
        ),
        cost_estimate=pl.CostEstimate(
            flops=flops, bytes_accessed=4 * rows * depth * orbitals, transcendentals=0
        ),
        name="pull_blocks",
    )(mask, side, ham, slope, cotangent, previous, head, tail)


def local(term_now, term_prev, cotangent, ham_blocks, block_mask, ham_slope, atom_owner):
    rows, slots, share, orbitals = ham_blocks.shape
    columns = term_now.shape[2]
    reach = (slots - 1) // 2
    edge = reach * share
    half = rows // 2
    ham = ham_blocks.reshape(rows, slots * share, orbitals)
    slope = ham_slope.reshape(rows, slots * share, orbitals)
    term = term_now.reshape(rows * share, columns)
    side = lax.axis_index("layers").astype(jnp.int32).reshape(1)

    below = shifted(term[rows * share - edge :], "rows", 1)
    above = shifted(term[:edge], "rows", -1)

    to_below, own, to_above = push(ham, block_mask, cotangent, share)
    from_above = shifted(to_below, "rows", -1)
    from_below = shifted(to_above, "rows", 1)

    args = (ham, slope, block_mask, side, cotangent, term_prev)
    keep_a, send_a, force_a = pull(*args, below, term, share, 0, half)
    got_a = swapped(send_a, "layers", 1)
    keep_b, send_b, force_b = pull(*args, term, above, share, half, rows - half)
    got_b = swapped(send_b, "layers", 1)

    row_force = jnp.concatenate([force_a, force_b], axis=0).reshape(rows, orbitals)
    atom_ids = lax.broadcasted_iota(jnp.int32, (1, 1, APB), 2)
    owned = jnp.where(atom_owner[:, :, None] == atom_ids, row_force[:, :, None], 0.0)
    forces = jnp.sum(owned, axis=1)
    forces = forces + swapped(forces, "layers", 1)
    bit = 1
    while bit < lax.axis_size("cols"):
        forces = forces + swapped(forces, "cols", bit)
        bit *= 2

    term_next = jnp.concatenate(
        [keep_a + got_a.astype(jnp.float32), keep_b + got_b.astype(jnp.float32)], axis=0
    ).astype(jnp.bfloat16)
    own = own.reshape(rows, share, columns)
    got = jnp.concatenate([from_below, from_above], axis=0).reshape(rows, share, columns)
    grad_term = (own + got.astype(jnp.float32)).astype(jnp.bfloat16)
    return (term_next, grad_term, forces)


def solution(mesh):
    return jax.shard_map(
        local,
        mesh=mesh,
        in_specs=(
            P("rows", "layers", "cols"),
            P("rows", "layers", "cols"),
            P("rows", None, "cols"),
            P("rows", None, "layers", None),
            P("rows", None),
            P("rows", None, "layers", None),
            P("rows", None),
        ),
        out_specs=(P("rows", "layers", "cols"), P("rows", "layers", "cols"), P("rows", None)),
        check_vma=False,
    )
```

```python
import functools

import jax
import jax.numpy as jnp
from jax import lax
from jax.experimental import pallas as pl
from jax.experimental.pallas import tpu as pltpu
from jax.sharding import PartitionSpec as P

APB = 64
VMEM_BYTES = 56 * 1024 * 1024
ARBITRARY = pltpu.GridDimensionSemantics.ARBITRARY


def shifted(value, axis, steps):
    count = lax.axis_size(axis)
    pairs = [(source, (source + steps) % count) for source in range(count)]
    return lax.ppermute(value, axis, pairs)


def swapped(value, axis, bit):
    count = lax.axis_size(axis)
    return lax.ppermute(value, axis, [(source, source ^ bit) for source in range(count)])


def push_kernel(
    group, sets, slots, share, mask_ref, ham_ref, cot_ref, edge_ref, low_ref, own_ref, high_ref, copy_ref, left, total
):
    step = pl.program_id(0)
    orbitals = ham_ref.shape[2]
    columns = cot_ref.shape[2]
    spread = (slots + group - 1) * share

    @pl.when(step == 0)
    def _():
        total[...] = jnp.zeros_like(total)
        left[...] = jnp.zeros_like(left)
        copy_ref[...] = edge_ref[...]

    for part in range(sets):
        base = part * group
        for k in range(group):
            row = step * (sets * group) + base + k
            for slot in range(slots):
                kept = mask_ref[row, slot] != 0
                block = ham_ref[base + k, slot * share : (slot + 1) * share, :]
                at = (slot + k) * share
                left[part, at : at + share, k * orbitals : (k + 1) * orbitals] = jnp.where(
                    kept, block, jnp.zeros_like(block)
                )
        right = cot_ref[base : base + group].reshape(group * orbitals, columns)
        first = pl.multiple_of((step * sets + part) * (group * share), group * share)
        piece = 2 * share
        for at in range(0, spread, piece):
            size = min(piece, spread - at)
            total[pl.ds(first + at, size), :] += jnp.dot(
                left[part, at : at + size, :], right, preferred_element_type=jnp.float32
            )

    @pl.when(step == pl.num_programs(0) - 1)
    def _():
        halo = low_ref.shape[0]
        own = own_ref.shape[0]
        low_ref[...] = (2.0 * total[:halo, :]).astype(low_ref.dtype)
        own_ref[...] = 2.0 * total[halo : halo + own, :]
        high_ref[...] = (2.0 * total[halo + own :, :]).astype(high_ref.dtype)


def largest_divisor(count, limit):
    return max(k for k in range(1, limit + 1) if count % k == 0)


def push(ham, mask, cotangent, term, share):
    rows, depth, orbitals = ham.shape
    columns = cotangent.shape[2]
    slots = depth // share
    reach = (slots - 1) // 2
    group = largest_divisor(rows, 2)
    sets = largest_divisor(rows // group, 2)
    each = group * sets
    kernel = functools.partial(push_kernel, group, sets, slots, share)
    flops = 2 * rows * depth * orbitals * columns
    edge = pl.BlockSpec((reach * share, columns), lambda i, m: (0, 0))
    return pl.pallas_call(
        kernel,
        out_shape=(
            jax.ShapeDtypeStruct((reach * share, columns), jnp.bfloat16),
            jax.ShapeDtypeStruct((rows * share, columns), jnp.float32),
            jax.ShapeDtypeStruct((reach * share, columns), jnp.bfloat16),
            jax.ShapeDtypeStruct((reach * share, columns), term.dtype),
        ),
        grid_spec=pltpu.PrefetchScalarGridSpec(
            num_scalar_prefetch=1,
            grid=(rows // each,),
            in_specs=[
                pl.BlockSpec((each, depth, orbitals), lambda i, m: (i, 0, 0)),
                pl.BlockSpec((each, orbitals, columns), lambda i, m: (i, 0, 0)),
                edge,
            ],
            out_specs=[edge, pl.BlockSpec((rows * share, columns), lambda i, m: (0, 0)), edge, edge],
            scratch_shapes=[
                pltpu.VMEM((sets, (slots + group - 1) * share, group * orbitals), jnp.bfloat16),
                pltpu.VMEM(((rows + 2 * reach) * share, columns), jnp.float32),
            ],
        ),
        compiler_params=pltpu.CompilerParams(
            dimension_semantics=(ARBITRARY,), vmem_limit_bytes=VMEM_BYTES
        ),
        cost_estimate=pl.CostEstimate(flops=flops, bytes_accessed=ham.size * 2, transcendentals=0),
        name="push_blocks",
    )(mask, ham, cotangent, term)


def pull_kernel(
    first_row, each, carried, slots, share, mask_ref, side_ref, ham_ref, slope_ref, cot_ref, prev_ref, head_ref, tail_ref, *rest,
):
    keep_ref, send_ref, force_ref = rest[carried : carried + 3]
    window, both, product = rest[-3:]
    step = pl.program_id(0)
    orbitals = ham_ref.shape[2]
    side = side_ref[0]

    @pl.when(step == 0)
    def _():
        split = head_ref.shape[0]
        window[:split, :] = head_ref[...]
        window[split:, :] = tail_ref[...]

    mine = pl.multiple_of(side * share, share)
    other = pl.multiple_of((1 - side) * share, share)
    for k in range(each):
        at = step * each + k
        row = first_row + at
        for slot in range(slots):
            kept = mask_ref[row, slot] != 0
            span = slice(slot * share, (slot + 1) * share)
            block = ham_ref[k, span, :]
            both[k, span, :orbitals] = jnp.where(kept, block, jnp.zeros_like(block))
            block = slope_ref[k, span, :]
            both[k, span, orbitals:] = jnp.where(kept, block, jnp.zeros_like(block))
        near = window[pl.ds(pl.multiple_of(at * share, share), slots * share), :]
        product[k] = lax.dot_general(
            both[k], near, (((0,), (0,)), ((), ())), preferred_element_type=jnp.float32
        )
        keep_ref[k] = 2.0 * product[k, pl.ds(mine, share), :] - prev_ref[k].astype(jnp.float32)
        send_ref[k] = (2.0 * product[k, pl.ds(other, share), :]).astype(send_ref.dtype)
        work = product[k, orbitals:, :] * cot_ref[k].astype(jnp.float32)
        lanes = 128
        folded = work[:, :lanes]
        for lane in range(lanes, work.shape[1], lanes):
            folded = folded + work[:, lane : lane + lanes]
        force_ref[k] = 2.0 * jnp.sum(folded.T, axis=0, keepdims=True)


def pull(ham, slope, mask, side, cotangent, previous, head, tail, share, first_row, rows, carried, keep):
    total_rows, depth, orbitals = ham.shape
    columns = cotangent.shape[2]
    slots = depth // share
    each = largest_divisor(rows, 3)
    skip = first_row // each
    assert skip * each == first_row
    held = tuple(carried) + ((keep,) if keep is not None else ())
    kernel = functools.partial(pull_kernel, first_row, each, len(held) + len(carried), slots, share)
    flops = 4 * rows * depth * orbitals * columns
    row_block = lambda *dims: pl.BlockSpec((each,) + dims, lambda i, m, s: (i + skip, 0, 0))
    whole = lambda a: pl.BlockSpec(a.shape, lambda i, m, s: (0, 0))
    out_block = lambda *dims: pl.BlockSpec((each,) + dims, lambda i, m, s: (i, 0, 0))
    anywhere = pl.BlockSpec(memory_space=pl.ANY)
    inputs = (mask, side, ham, slope, cotangent, previous, head, tail)
    aliases = {len(inputs) + k: k for k in range(len(held))}
    return pl.pallas_call(
        kernel,
        out_shape=tuple(jax.ShapeDtypeStruct(a.shape, a.dtype) for a in carried)
        + (
            jax.ShapeDtypeStruct((total_rows, share, columns), jnp.float32),
            jax.ShapeDtypeStruct((rows, share, columns), jnp.bfloat16),
            jax.ShapeDtypeStruct((rows, 1, orbitals), jnp.float32),
        ),
        grid_spec=pltpu.PrefetchScalarGridSpec(
            num_scalar_prefetch=2,
            grid=(rows // each,),
            in_specs=[
                row_block(depth, orbitals),
                row_block(depth, orbitals),
                row_block(orbitals, columns),
                row_block(share, columns),
                whole(head),
                whole(tail),
            ]
            + [anywhere] * len(held),
            out_specs=[anywhere] * len(carried)
            + [
                row_block(share, columns),
                out_block(share, columns),
                out_block(1, orbitals),
            ],
            scratch_shapes=[
                pltpu.VMEM((head.shape[0] + tail.shape[0], columns), jnp.bfloat16),
                pltpu.VMEM((each, depth, 2 * orbitals), jnp.bfloat16),
                pltpu.VMEM((each, 2 * orbitals, columns), jnp.float32),
            ],
        ),
        input_output_aliases=aliases,
        compiler_params=pltpu.CompilerParams(
            dimension_semantics=(ARBITRARY,), vmem_limit_bytes=VMEM_BYTES
        ),
        cost_estimate=pl.CostEstimate(
            flops=flops, bytes_accessed=4 * rows * depth * orbitals, transcendentals=0
        ),
        name="pull_blocks",
    )(*inputs, *held)


def local(term_now, term_prev, cotangent, ham_blocks, block_mask, ham_slope, atom_owner):
    rows, slots, share, orbitals = ham_blocks.shape
    columns = term_now.shape[2]
    reach = (slots - 1) // 2
    edge = reach * share
    half = rows // 2
    ham = ham_blocks.reshape(rows, slots * share, orbitals)
    slope = ham_slope.reshape(rows, slots * share, orbitals)
    term = term_now.reshape(rows * share, columns)
    side = lax.axis_index("layers").astype(jnp.int32).reshape(1)

    below = shifted(term[rows * share - edge :], "rows", 1)
    to_below, own, to_above, first_edge = push(ham, block_mask, cotangent, term, share)
    above = shifted(first_edge, "rows", -1)

    args = (ham, slope, block_mask, side, cotangent, term_prev)
    to_below, to_above, keep, send_a, force_a = pull(
        *args, below, term, share, 0, half, (to_below, to_above), None
    )
    from_above = shifted(to_below, "rows", -1)
    from_below = shifted(to_above, "rows", 1)
    got_a = swapped(send_a, "layers", 1)
    keep, send_b, force_b = pull(*args, term, above, share, half, rows - half, (), keep)
    got_b = swapped(send_b, "layers", 1)

    row_force = jnp.concatenate([force_a, force_b], axis=0).reshape(rows, orbitals)
    atom_ids = lax.broadcasted_iota(jnp.int32, (1, 1, APB), 2)
    owned = jnp.where(atom_owner[:, :, None] == atom_ids, row_force[:, :, None], 0.0)
    forces = jnp.sum(owned, axis=1)
    forces = forces + swapped(forces, "layers", 1)
    bit = 1
    while bit < lax.axis_size("cols"):
        forces = forces + swapped(forces, "cols", bit)
        bit *= 2

    got = jnp.concatenate([got_a, got_b], axis=0)
    term_next = (keep + got.astype(jnp.float32)).astype(jnp.bfloat16)
    own = own.reshape(rows, share, columns)
    got = jnp.concatenate([from_below, from_above], axis=0).reshape(rows, share, columns)
    grad_term = (own + got.astype(jnp.float32)).astype(jnp.bfloat16)
    return (term_next, grad_term, forces)


def solution(mesh):
    return jax.shard_map(
        local,
        mesh=mesh,
        in_specs=(
            P("rows", "layers", "cols"),
            P("rows", "layers", "cols"),
            P("rows", None, "cols"),
            P("rows", None, "layers", None),
            P("rows", None),
            P("rows", None, "layers", None),
            P("rows", None),
        ),
        out_specs=(P("rows", "layers", "cols"), P("rows", "layers", "cols"), P("rows", None)),
        check_vma=False,
    )
```

```python
import functools

import jax
import jax.numpy as jnp
from jax import lax
from jax.experimental import pallas as pl
from jax.experimental.pallas import tpu as pltpu
from jax.sharding import PartitionSpec as P

APB = 64
VMEM_BYTES = 56 * 1024 * 1024
ARBITRARY = pltpu.GridDimensionSemantics.ARBITRARY


def shifted(value, axis, steps):
    count = lax.axis_size(axis)
    pairs = [(source, (source + steps) % count) for source in range(count)]
    return lax.ppermute(value, axis, pairs)


def swapped(value, axis, bit):
    count = lax.axis_size(axis)
    return lax.ppermute(value, axis, [(source, source ^ bit) for source in range(count)])


def push_kernel(
    group, sets, slots, share, mask_ref, ham_ref, cot_ref, edge_ref, low_ref, own_ref, high_ref, copy_ref, left, total
):
    step = pl.program_id(0)
    orbitals = ham_ref.shape[2]
    columns = cot_ref.shape[2]
    spread = (slots + group - 1) * share

    @pl.when(step == 0)
    def _():
        total[...] = jnp.zeros_like(total)
        left[...] = jnp.zeros_like(left)
        copy_ref[...] = edge_ref[...]

    for part in range(sets):
        base = part * group
        for k in range(group):
            row = step * (sets * group) + base + k
            for slot in range(slots):
                kept = mask_ref[row, slot] != 0
                block = ham_ref[base + k, slot * share : (slot + 1) * share, :]
                at = (slot + k) * share
                left[part, at : at + share, k * orbitals : (k + 1) * orbitals] = jnp.where(
                    kept, block, jnp.zeros_like(block)
                )
        right = cot_ref[base : base + group].reshape(group * orbitals, columns)
        first = pl.multiple_of((step * sets + part) * (group * share), group * share)
        piece = 2 * share
        for at in range(0, spread, piece):
            size = min(piece, spread - at)
            total[pl.ds(first + at, size), :] += jnp.dot(
                left[part, at : at + size, :], right, preferred_element_type=jnp.float32
            )

    @pl.when(step == pl.num_programs(0) - 1)
    def _():
        halo = low_ref.shape[0]
        own = own_ref.shape[0]
        low_ref[...] = (2.0 * total[:halo, :]).astype(low_ref.dtype)
        own_ref[...] = 2.0 * total[halo : halo + own, :]
        high_ref[...] = (2.0 * total[halo + own :, :]).astype(high_ref.dtype)


def largest_divisor(count, limit):
    return max(k for k in range(1, limit + 1) if count % k == 0)


def push(ham, mask, cotangent, term, share):
    rows, depth, orbitals = ham.shape
    columns = cotangent.shape[2]
    slots = depth // share
    reach = (slots - 1) // 2
    group = largest_divisor(rows, 2)
    sets = largest_divisor(rows // group, 2)
    each = group * sets
    kernel = functools.partial(push_kernel, group, sets, slots, share)
    flops = 2 * rows * depth * orbitals * columns
    edge = pl.BlockSpec((reach * share, columns), lambda i, m: (0, 0))
    return pl.pallas_call(
        kernel,
        out_shape=(
            jax.ShapeDtypeStruct((reach * share, columns), jnp.bfloat16),
            jax.ShapeDtypeStruct((rows * share, columns), jnp.float32),
            jax.ShapeDtypeStruct((reach * share, columns), jnp.bfloat16),
            jax.ShapeDtypeStruct((reach * share, columns), term.dtype),
        ),
        grid_spec=pltpu.PrefetchScalarGridSpec(
            num_scalar_prefetch=1,
            grid=(rows // each,),
            in_specs=[
                pl.BlockSpec((each, depth, orbitals), lambda i, m: (i, 0, 0)),
                pl.BlockSpec((each, orbitals, columns), lambda i, m: (i, 0, 0)),
                edge,
            ],
            out_specs=[edge, pl.BlockSpec((rows * share, columns), lambda i, m: (0, 0)), edge, edge],
            scratch_shapes=[
                pltpu.VMEM((sets, (slots + group - 1) * share, group * orbitals), jnp.bfloat16),
                pltpu.VMEM(((rows + 2 * reach) * share, columns), jnp.float32),
            ],
        ),
        compiler_params=pltpu.CompilerParams(
            dimension_semantics=(ARBITRARY,), vmem_limit_bytes=VMEM_BYTES
        ),
        cost_estimate=pl.CostEstimate(flops=flops, bytes_accessed=ham.size * 2, transcendentals=0),
        name="push_blocks",
    )(mask, ham, cotangent, term)


def pull_kernel(
    first_row, each, carried, slots, share, mask_ref, side_ref, ham_ref, slope_ref, cot_ref, prev_ref, head_ref, tail_ref, *rest,
):
    keep_ref, send_ref, force_ref = rest[carried : carried + 3]
    window, both, product = rest[-3:]
    step = pl.program_id(0)
    orbitals = ham_ref.shape[2]
    side = side_ref[0]

    @pl.when(step == 0)
    def _():
        split = head_ref.shape[0]
        window[:split, :] = head_ref[...]
        window[split:, :] = tail_ref[...]

    mine = pl.multiple_of(side * share, share)
    other = pl.multiple_of((1 - side) * share, share)
    for k in range(each):
        at = step * each + k
        row = first_row + at
        for slot in range(slots):
            kept = mask_ref[row, slot] != 0
            span = slice(slot * share, (slot + 1) * share)
            block = ham_ref[k, span, :]
            both[k, span, :orbitals] = jnp.where(kept, block, jnp.zeros_like(block))
            block = slope_ref[k, span, :]
            both[k, span, orbitals:] = jnp.where(kept, block, jnp.zeros_like(block))
        near = window[pl.ds(pl.multiple_of(at * share, share), slots * share), :]
        product[k] = lax.dot_general(
            both[k], near, (((0,), (0,)), ((), ())), preferred_element_type=jnp.float32
        )
        keep_ref[k] = 2.0 * product[k, pl.ds(mine, share), :] - prev_ref[k].astype(jnp.float32)
        send_ref[k] = (2.0 * product[k, pl.ds(other, share), :]).astype(send_ref.dtype)
        work = product[k, orbitals:, :] * cot_ref[k].astype(jnp.float32)
        lanes = 128
        folded = work[:, :lanes]
        for lane in range(lanes, work.shape[1], lanes):
            folded = folded + work[:, lane : lane + lanes]
        force_ref[k] = 2.0 * jnp.sum(folded.T, axis=0, keepdims=True)


def pull(ham, slope, mask, side, cotangent, previous, head, tail, share, first_row, rows, carried, keep):
    total_rows, depth, orbitals = ham.shape
    columns = cotangent.shape[2]
    slots = depth // share
    each = largest_divisor(rows, 3)
    skip = first_row // each
    assert skip * each == first_row
    held = tuple(carried) + ((keep,) if keep is not None else ())
    kernel = functools.partial(pull_kernel, first_row, each, len(held) + len(carried), slots, share)
    flops = 4 * rows * depth * orbitals * columns
    row_block = lambda *dims: pl.BlockSpec((each,) + dims, lambda i, m, s: (i + skip, 0, 0))
    whole = lambda a: pl.BlockSpec(a.shape, lambda i, m, s: (0, 0))
    out_block = lambda *dims: pl.BlockSpec((each,) + dims, lambda i, m, s: (i, 0, 0))
    anywhere = pl.BlockSpec(memory_space=pl.ANY)
    inputs = (mask, side, ham, slope, cotangent, previous, head, tail)
    aliases = {len(inputs) + k: k for k in range(len(held))}
    return pl.pallas_call(
        kernel,
        out_shape=tuple(jax.ShapeDtypeStruct(a.shape, a.dtype) for a in carried)
        + (
            jax.ShapeDtypeStruct((total_rows, share, columns), jnp.float32),
            jax.ShapeDtypeStruct((rows, share, columns), jnp.bfloat16),
            jax.ShapeDtypeStruct((rows, 1, orbitals), jnp.float32),
        ),
        grid_spec=pltpu.PrefetchScalarGridSpec(
            num_scalar_prefetch=2,
            grid=(rows // each,),
            in_specs=[
                row_block(depth, orbitals),
                row_block(depth, orbitals),
                row_block(orbitals, columns),
                row_block(share, columns),
                whole(head),
                whole(tail),
            ]
            + [anywhere] * len(held),
            out_specs=[anywhere] * len(carried)
            + [
                row_block(share, columns),
                out_block(share, columns),
                out_block(1, orbitals),
            ],
            scratch_shapes=[
                pltpu.VMEM((head.shape[0] + tail.shape[0], columns), jnp.bfloat16),
                pltpu.VMEM((each, depth, 2 * orbitals), jnp.bfloat16),
                pltpu.VMEM((each, 2 * orbitals, columns), jnp.float32),
            ],
        ),
        input_output_aliases=aliases,
        compiler_params=pltpu.CompilerParams(
            dimension_semantics=(ARBITRARY,), vmem_limit_bytes=VMEM_BYTES
        ),
        cost_estimate=pl.CostEstimate(
            flops=flops, bytes_accessed=4 * rows * depth * orbitals, transcendentals=0
        ),
        name="pull_blocks",
    )(*inputs, *held)


def local(term_now, term_prev, cotangent, ham_blocks, block_mask, ham_slope, atom_owner):
    rows, slots, share, orbitals = ham_blocks.shape
    columns = term_now.shape[2]
    reach = (slots - 1) // 2
    edge = reach * share
    half = rows // 2
    ham = ham_blocks.reshape(rows, slots * share, orbitals)
    slope = ham_slope.reshape(rows, slots * share, orbitals)
    term = term_now.reshape(rows * share, columns)
    side = lax.axis_index("layers").astype(jnp.int32).reshape(1)

    below = shifted(term[rows * share - edge :], "rows", 1)
    to_below, own, to_above, first_edge = push(ham, block_mask, cotangent, term, share)
    above = shifted(first_edge, "rows", -1)

    args = (ham, slope, block_mask, side, cotangent, term_prev)
    to_below, to_above, keep, send_a, force_a = pull(
        *args, below, term, share, 0, half, (to_below, to_above), None
    )
    from_above = shifted(to_below, "rows", -1)
    from_below = shifted(to_above, "rows", 1)
    got_a = swapped(send_a, "layers", 1)
    paired = 2 if lax.axis_size("cols") % 2 == 0 else 1
    if paired == 2:
        force_a = force_a + swapped(force_a, "cols", 1)
    force_a, keep, send_b, force_b = pull(
        *args, term, above, share, half, rows - half, (force_a,), keep
    )
    got_b = swapped(send_b, "layers", 1)

    force_b, got_a = lax.optimization_barrier((force_b, got_a))
    row_force = jnp.concatenate([force_a, force_b], axis=0).reshape(rows, orbitals)
    atom_ids = lax.broadcasted_iota(jnp.int32, (1, 1, APB), 2)
    owned = jnp.where(atom_owner[:, :, None] == atom_ids, row_force[:, :, None], 0.0)
    forces = jnp.sum(owned, axis=1)
    gathered = lax.all_gather(forces, "cols")
    forces = jnp.concatenate(
        [jnp.sum(gathered[::paired, :half], axis=0), jnp.sum(gathered[:, half:], axis=0)], axis=0
    )
    forces = forces + swapped(forces, "layers", 1)
    got_b, from_below, from_above, forces = lax.optimization_barrier((got_b, from_below, from_above, forces))
    got = jnp.concatenate([got_a, got_b], axis=0)
    term_next = (keep + got.astype(jnp.float32)).astype(jnp.bfloat16)
    own = own.reshape(rows, share, columns)
    got = jnp.concatenate([from_below, from_above], axis=0).reshape(rows, share, columns)
    grad_term = (own + got.astype(jnp.float32)).astype(jnp.bfloat16)
    return (term_next, grad_term, forces)


def solution(mesh):
    return jax.shard_map(
        local,
        mesh=mesh,
        in_specs=(
            P("rows", "layers", "cols"),
            P("rows", "layers", "cols"),
            P("rows", None, "cols"),
            P("rows", None, "layers", None),
            P("rows", None),
            P("rows", None, "layers", None),
            P("rows", None),
        ),
        out_specs=(P("rows", "layers", "cols"), P("rows", "layers", "cols"), P("rows", None)),
        check_vma=False,
    )
```

```python
import functools

import jax
import jax.numpy as jnp
from jax import lax
from jax.experimental import pallas as pl
from jax.experimental.pallas import tpu as pltpu
from jax.sharding import PartitionSpec as P

APB = 64
VMEM_BYTES = 56 * 1024 * 1024
ARBITRARY = pltpu.GridDimensionSemantics.ARBITRARY


def shifted(value, axis, steps):
    count = lax.axis_size(axis)
    pairs = [(source, (source + steps) % count) for source in range(count)]
    return lax.ppermute(value, axis, pairs)


def swapped(value, axis, bit):
    count = lax.axis_size(axis)
    return lax.ppermute(value, axis, [(source, source ^ bit) for source in range(count)])


def push_kernel(
    group, sets, slots, share, mask_ref, ham_ref, cot_ref, edge_ref, low_ref, own_ref, high_ref, copy_ref, left, total
):
    step = pl.program_id(0)
    orbitals = ham_ref.shape[2]
    columns = cot_ref.shape[2]
    spread = (slots + group - 1) * share

    @pl.when(step == 0)
    def _():
        total[...] = jnp.zeros_like(total)
        left[...] = jnp.zeros_like(left)
        copy_ref[...] = edge_ref[...]

    for part in range(sets):
        base = part * group
        for k in range(group):
            row = step * (sets * group) + base + k
            for slot in range(slots):
                kept = mask_ref[row, slot] != 0
                block = ham_ref[base + k, slot * share : (slot + 1) * share, :]
                at = (slot + k) * share
                left[part, at : at + share, k * orbitals : (k + 1) * orbitals] = jnp.where(
                    kept, block, jnp.zeros_like(block)
                )
        right = cot_ref[base : base + group].reshape(group * orbitals, columns)
        first = pl.multiple_of((step * sets + part) * (group * share), group * share)
        piece = 2 * share
        for at in range(0, spread, piece):
            size = min(piece, spread - at)
            total[pl.ds(first + at, size), :] += jnp.dot(
                left[part, at : at + size, :], right, preferred_element_type=jnp.float32
            )

    @pl.when(step == pl.num_programs(0) - 1)
    def _():
        halo = low_ref.shape[0]
        own = own_ref.shape[0]
        low_ref[...] = (2.0 * total[:halo, :]).astype(low_ref.dtype)
        own_ref[...] = 2.0 * total[halo : halo + own, :]
        high_ref[...] = (2.0 * total[halo + own :, :]).astype(high_ref.dtype)


def largest_divisor(count, limit):
    return max(k for k in range(1, limit + 1) if count % k == 0)


def push(ham, mask, cotangent, term, share):
    rows, depth, orbitals = ham.shape
    columns = cotangent.shape[2]
    slots = depth // share
    reach = (slots - 1) // 2
    group = largest_divisor(rows, 2)
    sets = largest_divisor(rows // group, 2)
    each = group * sets
    kernel = functools.partial(push_kernel, group, sets, slots, share)
    flops = 2 * rows * depth * orbitals * columns
    edge = pl.BlockSpec((reach * share, columns), lambda i, m: (0, 0))
    return pl.pallas_call(
        kernel,
        out_shape=(
            jax.ShapeDtypeStruct((reach * share, columns), jnp.bfloat16),
            jax.ShapeDtypeStruct((rows * share, columns), jnp.float32),
            jax.ShapeDtypeStruct((reach * share, columns), jnp.bfloat16),
            jax.ShapeDtypeStruct((reach * share, columns), term.dtype),
        ),
        grid_spec=pltpu.PrefetchScalarGridSpec(
            num_scalar_prefetch=1,
            grid=(rows // each,),
            in_specs=[
                pl.BlockSpec((each, depth, orbitals), lambda i, m: (i, 0, 0)),
                pl.BlockSpec((each, orbitals, columns), lambda i, m: (i, 0, 0)),
                edge,
            ],
            out_specs=[edge, pl.BlockSpec((rows * share, columns), lambda i, m: (0, 0)), edge, edge],
            scratch_shapes=[
                pltpu.VMEM((sets, (slots + group - 1) * share, group * orbitals), jnp.bfloat16),
                pltpu.VMEM(((rows + 2 * reach) * share, columns), jnp.float32),
            ],
        ),
        compiler_params=pltpu.CompilerParams(
            dimension_semantics=(ARBITRARY,), vmem_limit_bytes=VMEM_BYTES
        ),
        cost_estimate=pl.CostEstimate(flops=flops, bytes_accessed=ham.size * 2, transcendentals=0),
        name="push_blocks",
    )(mask, ham, cotangent, term)


def pull_kernel(
    first_row, each, carried, slots, share, mask_ref, side_ref, ham_ref, slope_ref, cot_ref, prev_ref, head_ref, tail_ref, *rest,
):
    keep_ref, send_ref, force_ref = rest[carried : carried + 3]
    window, both, product = rest[-3:]
    step = pl.program_id(0)
    orbitals = ham_ref.shape[2]
    side = side_ref[0]

    @pl.when(step == 0)
    def _():
        split = head_ref.shape[0]
        window[:split, :] = head_ref[...]
        window[split:, :] = tail_ref[...]

    mine = pl.multiple_of(side * share, share)
    other = pl.multiple_of((1 - side) * share, share)
    for k in range(each):
        at = step * each + k
        row = first_row + at
        for slot in range(slots):
            kept = mask_ref[row, slot] != 0
            span = slice(slot * share, (slot + 1) * share)
            block = ham_ref[k, span, :]
            both[k, span, :orbitals] = jnp.where(kept, block, jnp.zeros_like(block))
            block = slope_ref[k, span, :]
            both[k, span, orbitals:] = jnp.where(kept, block, jnp.zeros_like(block))
        near = window[pl.ds(pl.multiple_of(at * share, share), slots * share), :]
        product[k] = lax.dot_general(
            both[k], near, (((0,), (0,)), ((), ())), preferred_element_type=jnp.float32
        )
        keep_ref[k] = 2.0 * product[k, pl.ds(mine, share), :] - prev_ref[k].astype(jnp.float32)
        send_ref[k] = (2.0 * product[k, pl.ds(other, share), :]).astype(send_ref.dtype)
        work = product[k, orbitals:, :] * cot_ref[k].astype(jnp.float32)
        lanes = 128
        folded = work[:, :lanes]
        for lane in range(lanes, work.shape[1], lanes):
            folded = folded + work[:, lane : lane + lanes]
        force_ref[k] = 2.0 * jnp.sum(folded.T, axis=0, keepdims=True)


def pull(ham, slope, mask, side, cotangent, previous, head, tail, share, first_row, rows, carried, keep):
    total_rows, depth, orbitals = ham.shape
    columns = cotangent.shape[2]
    slots = depth // share
    each = largest_divisor(rows, 3)
    skip = first_row // each
    assert skip * each == first_row
    held = tuple(carried) + ((keep,) if keep is not None else ())
    kernel = functools.partial(pull_kernel, first_row, each, len(held) + len(carried), slots, share)
    flops = 4 * rows * depth * orbitals * columns
    row_block = lambda *dims: pl.BlockSpec((each,) + dims, lambda i, m, s: (i + skip, 0, 0))
    whole = lambda a: pl.BlockSpec(a.shape, lambda i, m, s: (0, 0))
    out_block = lambda *dims: pl.BlockSpec((each,) + dims, lambda i, m, s: (i, 0, 0))
    anywhere = pl.BlockSpec(memory_space=pl.ANY)
    inputs = (mask, side, ham, slope, cotangent, previous, head, tail)
    aliases = {len(inputs) + k: k for k in range(len(held))}
    return pl.pallas_call(
        kernel,
        out_shape=tuple(jax.ShapeDtypeStruct(a.shape, a.dtype) for a in carried)
        + (
            jax.ShapeDtypeStruct((total_rows, share, columns), jnp.float32),
            jax.ShapeDtypeStruct((rows, share, columns), jnp.bfloat16),
            jax.ShapeDtypeStruct((rows, 1, orbitals), jnp.float32),
        ),
        grid_spec=pltpu.PrefetchScalarGridSpec(
            num_scalar_prefetch=2,
            grid=(rows // each,),
            in_specs=[
                row_block(depth, orbitals),
                row_block(depth, orbitals),
                row_block(orbitals, columns),
                row_block(share, columns),
                whole(head),
                whole(tail),
            ]
            + [anywhere] * len(held),
            out_specs=[anywhere] * len(carried)
            + [
                row_block(share, columns),
                out_block(share, columns),
                out_block(1, orbitals),
            ],
            scratch_shapes=[
                pltpu.VMEM((head.shape[0] + tail.shape[0], columns), jnp.bfloat16),
                pltpu.VMEM((each, depth, 2 * orbitals), jnp.bfloat16),
                pltpu.VMEM((each, 2 * orbitals, columns), jnp.float32),
            ],
        ),
        input_output_aliases=aliases,
        compiler_params=pltpu.CompilerParams(
            dimension_semantics=(ARBITRARY,), vmem_limit_bytes=VMEM_BYTES
        ),
        cost_estimate=pl.CostEstimate(
            flops=flops, bytes_accessed=4 * rows * depth * orbitals, transcendentals=0
        ),
        name="pull_blocks",
    )(*inputs, *held)


def add_kernel(steps, own_ref, first_ref, second_ref, *rest):
    out_ref = rest[-1]
    step = pl.program_id(0)

    @pl.when(step < steps)
    def _():
        out_ref[...] = (own_ref[...] + first_ref[...].astype(jnp.float32)).astype(out_ref.dtype)

    @pl.when(step >= steps)
    def _():
        out_ref[...] = (own_ref[...] + second_ref[...].astype(jnp.float32)).astype(out_ref.dtype)


def add_parts(own, arrived, size, places, filled):
    columns = own.shape[1]
    steps = 2
    piece = size // steps
    (one, one_at), (two, two_at) = arrived

    def spec(first_at, second_at, turn):
        def place(i):
            near = jnp.minimum(i, steps - 1) if turn == 0 else i
            far = jnp.maximum(i - steps, 0)
            if turn == 0:
                return (first_at * steps + near, 0)
            if turn == 1:
                return (second_at * steps + far, 0)
            return (jnp.where(i < steps, first_at * steps + i, second_at * steps + i - steps), 0)

        return pl.BlockSpec((piece, columns), place)

    held = () if filled is None else (filled,)
    return pl.pallas_call(
        functools.partial(add_kernel, steps),
        out_shape=jax.ShapeDtypeStruct(own.shape, jnp.bfloat16),
        grid=(2 * steps,),
        in_specs=[spec(*places, 2), spec(one_at, 0, 0), spec(0, two_at, 1)]
        + [pl.BlockSpec(memory_space=pl.ANY)] * len(held),
        out_specs=spec(*places, 2),
        input_output_aliases={3: 0} if held else {},
        compiler_params=pltpu.CompilerParams(
            dimension_semantics=(ARBITRARY,), vmem_limit_bytes=8 * 1024 * 1024
        ),
        cost_estimate=pl.CostEstimate(flops=0, bytes_accessed=0, transcendentals=0),
        name="add_parts",
    )(own, one, two, *held)


def local(term_now, term_prev, cotangent, ham_blocks, block_mask, ham_slope, atom_owner):
    rows, slots, share, orbitals = ham_blocks.shape
    columns = term_now.shape[2]
    reach = (slots - 1) // 2
    edge = reach * share
    half = rows // 2
    ham = ham_blocks.reshape(rows, slots * share, orbitals)
    slope = ham_slope.reshape(rows, slots * share, orbitals)
    term = term_now.reshape(rows * share, columns)
    side = lax.axis_index("layers").astype(jnp.int32).reshape(1)

    below = shifted(term[rows * share - edge :], "rows", 1)
    to_below, own, to_above, first_edge = push(ham, block_mask, cotangent, term, share)
    above = shifted(first_edge, "rows", -1)

    args = (ham, slope, block_mask, side, cotangent, term_prev)
    to_above, keep, send_a, force_a = pull(*args, below, term, share, 0, half, (to_above,), None)
    from_below = shifted(to_above, "rows", 1)
    got_a = swapped(send_a, "layers", 1)
    paired = 2 if lax.axis_size("cols") % 2 == 0 else 1
    if paired == 2:
        force_a = force_a + swapped(force_a, "cols", 1)
    force_a, to_below, keep, send_b, force_b = pull(
        *args, term, above, share, half, rows - half, (force_a, to_below), keep
    )
    got_b = swapped(send_b, "layers", 1)
    from_above = shifted(to_below, "rows", -1)

    row_force = jnp.concatenate([force_a, force_b], axis=0).reshape(rows, orbitals)
    atom_ids = lax.broadcasted_iota(jnp.int32, (1, 1, APB), 2)
    owned = jnp.where(atom_owner[:, :, None] == atom_ids, row_force[:, :, None], 0.0)
    forces = jnp.sum(owned, axis=1)
    gathered = lax.all_gather(forces, "cols")
    forces = jnp.concatenate(
        [jnp.sum(gathered[::paired, :half], axis=0), jnp.sum(gathered[:, half:], axis=0)], axis=0
    )
    others = swapped(forces, "layers", 1)

    keep = keep.reshape(rows * share, columns)
    got_a = got_a.reshape(half * share, columns)
    got_b = got_b.reshape((rows - half) * share, columns)
    size = edge // 2
    term_next = add_parts(keep, ((got_a, 0), (got_a, 1)), size, (0, 1), None)
    from_below, term_next = lax.optimization_barrier((from_below, term_next))
    grad_term = add_parts(own, ((from_below, 0), (from_below, 1)), size, (0, 1), None)
    got_b, grad_term = lax.optimization_barrier((got_b, grad_term))
    term_next = add_parts(keep, ((got_b, 0), (got_b, 1)), size, (2, 3), term_next)
    others, term_next = lax.optimization_barrier((others, term_next))
    forces = forces + others
    from_above, term_next, forces = lax.optimization_barrier((from_above, term_next, forces))
    grad_term = add_parts(own, ((from_above, 0), (from_above, 1)), size, (2, 3), grad_term)
    shape = (rows, share, columns)
    return (term_next.reshape(shape), grad_term.reshape(shape), forces)


def solution(mesh):
    return jax.shard_map(
        local,
        mesh=mesh,
        in_specs=(
            P("rows", "layers", "cols"),
            P("rows", "layers", "cols"),
            P("rows", None, "cols"),
            P("rows", None, "layers", None),
            P("rows", None),
            P("rows", None, "layers", None),
            P("rows", None),
        ),
        out_specs=(P("rows", "layers", "cols"), P("rows", "layers", "cols"), P("rows", None)),
        check_vma=False,
    )
```

```python
import functools

import jax
import jax.numpy as jnp
from jax import lax
from jax.experimental import pallas as pl
from jax.experimental.pallas import tpu as pltpu
from jax.sharding import PartitionSpec as P

APB = 64
VMEM_BYTES = 62 * 1024 * 1024
ARBITRARY = pltpu.GridDimensionSemantics.ARBITRARY


def shifted(value, axis, steps):
    count = lax.axis_size(axis)
    pairs = [(source, (source + steps) % count) for source in range(count)]
    return lax.ppermute(value, axis, pairs)


def swapped(value, axis, bit):
    count = lax.axis_size(axis)
    return lax.ppermute(value, axis, [(source, source ^ bit) for source in range(count)])


def push_kernel(
    group, sets, slots, share, mask_ref, ham_ref, cot_ref, edge_ref, low_ref, own_ref, high_ref, copy_ref, left, total
):
    step = pl.program_id(0)
    orbitals = ham_ref.shape[2]
    columns = cot_ref.shape[2]
    spread = (slots + group - 1) * share

    @pl.when(step == 0)
    def _():
        total[...] = jnp.zeros_like(total)
        left[...] = jnp.zeros_like(left)
        copy_ref[...] = edge_ref[...]

    for part in range(sets):
        base = part * group
        for k in range(group):
            row = step * (sets * group) + base + k
            for slot in range(slots):
                kept = mask_ref[row, slot] != 0
                block = ham_ref[base + k, slot * share : (slot + 1) * share, :]
                at = (slot + k) * share
                left[part, at : at + share, k * orbitals : (k + 1) * orbitals] = jnp.where(
                    kept, block, jnp.zeros_like(block)
                )
        right = cot_ref[base : base + group].reshape(group * orbitals, columns)
        first = pl.multiple_of((step * sets + part) * (group * share), group * share)
        piece = 2 * share
        for at in range(0, spread, piece):
            size = min(piece, spread - at)
            total[pl.ds(first + at, size), :] += jnp.dot(
                left[part, at : at + size, :], right, preferred_element_type=jnp.float32
            )

    @pl.when(step == pl.num_programs(0) - 1)
    def _():
        halo = low_ref.shape[0]
        own = own_ref.shape[0]
        low_ref[...] = (2.0 * total[:halo, :]).astype(low_ref.dtype)
        own_ref[...] = 2.0 * total[halo : halo + own, :]
        high_ref[...] = (2.0 * total[halo + own :, :]).astype(high_ref.dtype)


def largest_divisor(count, limit):
    return max(k for k in range(1, limit + 1) if count % k == 0)


def push(ham, mask, cotangent, term, share):
    rows, depth, orbitals = ham.shape
    columns = cotangent.shape[2]
    slots = depth // share
    reach = (slots - 1) // 2
    group = largest_divisor(rows, 6)
    sets = largest_divisor(rows // group, 2)
    each = group * sets
    kernel = functools.partial(push_kernel, group, sets, slots, share)
    flops = 2 * rows * depth * orbitals * columns
    edge = pl.BlockSpec((reach * share, columns), lambda i, m: (0, 0))
    return pl.pallas_call(
        kernel,
        out_shape=(
            jax.ShapeDtypeStruct((reach * share, columns), jnp.bfloat16),
            jax.ShapeDtypeStruct((rows * share, columns), jnp.float32),
            jax.ShapeDtypeStruct((reach * share, columns), jnp.bfloat16),
            jax.ShapeDtypeStruct((reach * share, columns), term.dtype),
        ),
        grid_spec=pltpu.PrefetchScalarGridSpec(
            num_scalar_prefetch=1,
            grid=(rows // each,),
            in_specs=[
                pl.BlockSpec((each, depth, orbitals), lambda i, m: (i, 0, 0)),
                pl.BlockSpec((each, orbitals, columns), lambda i, m: (i, 0, 0)),
                edge,
            ],
            out_specs=[edge, pl.BlockSpec((rows * share, columns), lambda i, m: (0, 0)), edge, edge],
            scratch_shapes=[
                pltpu.VMEM((sets, (slots + group - 1) * share, group * orbitals), jnp.bfloat16),
                pltpu.VMEM(((rows + 2 * reach) * share, columns), jnp.float32),
            ],
        ),
        compiler_params=pltpu.CompilerParams(
            dimension_semantics=(ARBITRARY,), vmem_limit_bytes=VMEM_BYTES
        ),
        cost_estimate=pl.CostEstimate(flops=flops, bytes_accessed=ham.size * 2, transcendentals=0),
        name="push_blocks",
    )(mask, ham, cotangent, term)


def pull_kernel(
    first_row, each, carried, slots, share, mask_ref, side_ref, ham_ref, slope_ref, cot_ref, prev_ref, head_ref, tail_ref, *rest,
):
    keep_ref, send_ref, force_ref = rest[carried : carried + 3]
    window, both, product = rest[-3:]
    step = pl.program_id(0)
    orbitals = ham_ref.shape[2]
    side = side_ref[0]

    @pl.when(step == 0)
    def _():
        split = head_ref.shape[0]
        window[:split, :] = head_ref[...]
        window[split:, :] = tail_ref[...]

    mine = pl.multiple_of(side * share, share)
    other = pl.multiple_of((1 - side) * share, share)
    for k in range(each):
        at = step * each + k
        row = first_row + at
        for slot in range(slots):
            kept = mask_ref[row, slot] != 0
            span = slice(slot * share, (slot + 1) * share)
            block = ham_ref[k, span, :]
            both[k, span, :orbitals] = jnp.where(kept, block, jnp.zeros_like(block))
            block = slope_ref[k, span, :]
            both[k, span, orbitals:] = jnp.where(kept, block, jnp.zeros_like(block))
        near = window[pl.ds(pl.multiple_of(at * share, share), slots * share), :]
        product[k] = lax.dot_general(
            both[k], near, (((0,), (0,)), ((), ())), preferred_element_type=jnp.float32
        )
        keep_ref[k] = 2.0 * product[k, pl.ds(mine, share), :] - prev_ref[k].astype(jnp.float32)
        send_ref[k] = (2.0 * product[k, pl.ds(other, share), :]).astype(send_ref.dtype)
        work = product[k, orbitals:, :] * cot_ref[k].astype(jnp.float32)
        lanes = 128
        folded = work[:, :lanes]
        for lane in range(lanes, work.shape[1], lanes):
            folded = folded + work[:, lane : lane + lanes]
        force_ref[k] = 2.0 * jnp.sum(folded.T, axis=0, keepdims=True)


def pull(ham, slope, mask, side, cotangent, previous, head, tail, share, first_row, rows, carried, keep):
    total_rows, depth, orbitals = ham.shape
    columns = cotangent.shape[2]
    slots = depth // share
    each = largest_divisor(rows, 3)
    skip = first_row // each
    assert skip * each == first_row
    held = tuple(carried) + ((keep,) if keep is not None else ())
    kernel = functools.partial(pull_kernel, first_row, each, len(held) + len(carried), slots, share)
    flops = 4 * rows * depth * orbitals * columns
    row_block = lambda *dims: pl.BlockSpec((each,) + dims, lambda i, m, s: (i + skip, 0, 0))
    whole = lambda a: pl.BlockSpec(a.shape, lambda i, m, s: (0, 0))
    out_block = lambda *dims: pl.BlockSpec((each,) + dims, lambda i, m, s: (i, 0, 0))
    anywhere = pl.BlockSpec(memory_space=pl.ANY)
    inputs = (mask, side, ham, slope, cotangent, previous, head, tail)
    aliases = {len(inputs) + k: k for k in range(len(held))}
    return pl.pallas_call(
        kernel,
        out_shape=tuple(jax.ShapeDtypeStruct(a.shape, a.dtype) for a in carried)
        + (
            jax.ShapeDtypeStruct((total_rows, share, columns), jnp.float32),
            jax.ShapeDtypeStruct((rows, share, columns), jnp.bfloat16),
            jax.ShapeDtypeStruct((rows, 1, orbitals), jnp.float32),
        ),
        grid_spec=pltpu.PrefetchScalarGridSpec(
            num_scalar_prefetch=2,
            grid=(rows // each,),
            in_specs=[
                row_block(depth, orbitals),
                row_block(depth, orbitals),
                row_block(orbitals, columns),
                row_block(share, columns),
                whole(head),
                whole(tail),
            ]
            + [anywhere] * len(held),
            out_specs=[anywhere] * len(carried)
            + [
                row_block(share, columns),
                out_block(share, columns),
                out_block(1, orbitals),
            ],
            scratch_shapes=[
                pltpu.VMEM((head.shape[0] + tail.shape[0], columns), jnp.bfloat16),
                pltpu.VMEM((each, depth, 2 * orbitals), jnp.bfloat16),
                pltpu.VMEM((each, 2 * orbitals, columns), jnp.float32),
            ],
        ),
        input_output_aliases=aliases,
        compiler_params=pltpu.CompilerParams(
            dimension_semantics=(ARBITRARY,), vmem_limit_bytes=VMEM_BYTES
        ),
        cost_estimate=pl.CostEstimate(
            flops=flops, bytes_accessed=4 * rows * depth * orbitals, transcendentals=0
        ),
        name="pull_blocks",
    )(*inputs, *held)


def add_kernel(steps, own_ref, first_ref, second_ref, *rest):
    out_ref = rest[-1]
    step = pl.program_id(0)

    @pl.when(step < steps)
    def _():
        out_ref[...] = (own_ref[...] + first_ref[...].astype(jnp.float32)).astype(out_ref.dtype)

    @pl.when(step >= steps)
    def _():
        out_ref[...] = (own_ref[...] + second_ref[...].astype(jnp.float32)).astype(out_ref.dtype)


def add_parts(own, arrived, size, places, filled):
    columns = own.shape[1]
    steps = 1
    piece = size // steps
    (one, one_at), (two, two_at) = arrived

    def spec(first_at, second_at, turn):
        def place(i):
            near = jnp.minimum(i, steps - 1) if turn == 0 else i
            far = jnp.maximum(i - steps, 0)
            if turn == 0:
                return (first_at * steps + near, 0)
            if turn == 1:
                return (second_at * steps + far, 0)
            return (jnp.where(i < steps, first_at * steps + i, second_at * steps + i - steps), 0)

        return pl.BlockSpec((piece, columns), place)

    held = () if filled is None else (filled,)
    return pl.pallas_call(
        functools.partial(add_kernel, steps),
        out_shape=jax.ShapeDtypeStruct(own.shape, jnp.bfloat16),
        grid=(2 * steps,),
        in_specs=[spec(*places, 2), spec(one_at, 0, 0), spec(0, two_at, 1)]
        + [pl.BlockSpec(memory_space=pl.ANY)] * len(held),
        out_specs=spec(*places, 2),
        input_output_aliases={3: 0} if held else {},
        compiler_params=pltpu.CompilerParams(
            dimension_semantics=(ARBITRARY,), vmem_limit_bytes=8 * 1024 * 1024
        ),
        cost_estimate=pl.CostEstimate(flops=0, bytes_accessed=0, transcendentals=0),
        name="add_parts",
    )(own, one, two, *held)


def local(term_now, term_prev, cotangent, ham_blocks, block_mask, ham_slope, atom_owner):
    rows, slots, share, orbitals = ham_blocks.shape
    columns = term_now.shape[2]
    reach = (slots - 1) // 2
    edge = reach * share
    half = rows // 2
    ham = ham_blocks.reshape(rows, slots * share, orbitals)
    slope = ham_slope.reshape(rows, slots * share, orbitals)
    term = term_now.reshape(rows * share, columns)
    side = lax.axis_index("layers").astype(jnp.int32).reshape(1)

    below = shifted(term[rows * share - edge :], "rows", 1)
    to_below, own, to_above, first_edge = push(ham, block_mask, cotangent, term, share)
    above = shifted(first_edge, "rows", -1)

    args = (ham, slope, block_mask, side, cotangent, term_prev)
    to_above, keep, send_a, force_a = pull(*args, below, term, share, 0, half, (to_above,), None)
    from_below = shifted(to_above, "rows", 1)
    got_a = swapped(send_a, "layers", 1)
    paired = 2 if lax.axis_size("cols") % 2 == 0 else 1
    other_a = swapped(force_a, "cols", 1) if paired == 2 else jnp.zeros_like(force_a)
    other_a, to_below, keep, send_b, force_b = pull(
        *args, term, above, share, half, rows - half, (other_a, to_below), keep
    )
    force_a = force_a + other_a
    got_b = swapped(send_b, "layers", 1)
    from_above = shifted(to_below, "rows", -1)

    row_force = jnp.concatenate([force_a, force_b], axis=0).reshape(rows, orbitals)
    atom_ids = lax.broadcasted_iota(jnp.int32, (1, 1, APB), 2)
    owned = jnp.where(atom_owner[:, :, None] == atom_ids, row_force[:, :, None], 0.0)
    forces = jnp.sum(owned, axis=1)
    gathered = lax.all_gather(forces, "cols")
    forces = jnp.concatenate(
        [jnp.sum(gathered[::paired, :half], axis=0), jnp.sum(gathered[:, half:], axis=0)], axis=0
    )
    others = swapped(forces, "layers", 1)

    keep = keep.reshape(rows * share, columns)
    got_a = got_a.reshape(half * share, columns)
    got_b = got_b.reshape((rows - half) * share, columns)
    size = edge // 2
    term_next = add_parts(keep, ((got_a, 0), (got_a, 1)), size, (0, 1), None)
    from_below, term_next = lax.optimization_barrier((from_below, term_next))
    grad_term = add_parts(own, ((from_below, 0), (from_below, 1)), size, (0, 1), None)
    got_b, grad_term = lax.optimization_barrier((got_b, grad_term))
    term_next = add_parts(keep, ((got_b, 0), (got_b, 1)), size, (2, 3), term_next)
    others, term_next = lax.optimization_barrier((others, term_next))
    forces = forces + others
    from_above, term_next, forces = lax.optimization_barrier((from_above, term_next, forces))
    grad_term = add_parts(own, ((from_above, 0), (from_above, 1)), size, (2, 3), grad_term)
    shape = (rows, share, columns)
    return (term_next.reshape(shape), grad_term.reshape(shape), forces)


def solution(mesh):
    return jax.shard_map(
        local,
        mesh=mesh,
        in_specs=(
            P("rows", "layers", "cols"),
            P("rows", "layers", "cols"),
            P("rows", None, "cols"),
            P("rows", None, "layers", None),
            P("rows", None),
            P("rows", None, "layers", None),
            P("rows", None),
        ),
        out_specs=(P("rows", "layers", "cols"), P("rows", "layers", "cols"), P("rows", None)),
        check_vma=False,
    )
```

```python
import functools

import jax
import jax.numpy as jnp
from jax import lax
from jax.experimental import pallas as pl
from jax.experimental.pallas import tpu as pltpu
from jax.sharding import PartitionSpec as P

APB = 64
VMEM_BYTES = 62 * 1024 * 1024
PULL_VMEM_BYTES = 51 * 1024 * 1024
ARBITRARY = pltpu.GridDimensionSemantics.ARBITRARY


def shifted(value, axis, steps):
    count = lax.axis_size(axis)
    pairs = [(source, (source + steps) % count) for source in range(count)]
    return lax.ppermute(value, axis, pairs)


def swapped(value, axis, bit):
    count = lax.axis_size(axis)
    return lax.ppermute(value, axis, [(source, source ^ bit) for source in range(count)])


def push_kernel(
    group, sets, slots, share, mask_ref, ham_ref, cot_ref, edge_ref, low_ref, own_ref, high_ref, copy_ref, left, total
):
    step = pl.program_id(0)
    orbitals = ham_ref.shape[2]
    columns = cot_ref.shape[2]
    spread = (slots + group - 1) * share

    @pl.when(step == 0)
    def _():
        total[...] = jnp.zeros_like(total)
        left[...] = jnp.zeros_like(left)
        copy_ref[...] = edge_ref[...]

    for part in range(sets):
        base = part * group
        for k in range(group):
            row = step * (sets * group) + base + k
            for slot in range(slots):
                kept = mask_ref[row, slot] != 0
                block = ham_ref[base + k, slot * share : (slot + 1) * share, :]
                at = (slot + k) * share
                left[part, at : at + share, k * orbitals : (k + 1) * orbitals] = jnp.where(
                    kept, block, jnp.zeros_like(block)
                )
        right = cot_ref[base : base + group].reshape(group * orbitals, columns)
        first = pl.multiple_of((step * sets + part) * (group * share), group * share)
        piece = 2 * share
        for at in range(0, spread, piece):
            size = min(piece, spread - at)
            total[pl.ds(first + at, size), :] += jnp.dot(
                left[part, at : at + size, :], right, preferred_element_type=jnp.float32
            )

    @pl.when(step == pl.num_programs(0) - 1)
    def _():
        halo = low_ref.shape[0]
        own = own_ref.shape[0]
        low_ref[...] = (2.0 * total[:halo, :]).astype(low_ref.dtype)
        own_ref[...] = 2.0 * total[halo : halo + own, :]
        high_ref[...] = (2.0 * total[halo + own :, :]).astype(high_ref.dtype)


def largest_divisor(count, limit):
    return max(k for k in range(1, limit + 1) if count % k == 0)


def push(ham, mask, cotangent, term, share):
    rows, depth, orbitals = ham.shape
    columns = cotangent.shape[2]
    slots = depth // share
    reach = (slots - 1) // 2
    group = largest_divisor(rows, 6)
    sets = largest_divisor(rows // group, 2)
    each = group * sets
    kernel = functools.partial(push_kernel, group, sets, slots, share)
    flops = 2 * rows * depth * orbitals * columns
    edge = pl.BlockSpec((reach * share, columns), lambda i, m: (0, 0))
    return pl.pallas_call(
        kernel,
        out_shape=(
            jax.ShapeDtypeStruct((reach * share, columns), jnp.bfloat16),
            jax.ShapeDtypeStruct((rows * share, columns), jnp.float32),
            jax.ShapeDtypeStruct((reach * share, columns), jnp.bfloat16),
            jax.ShapeDtypeStruct((reach * share, columns), term.dtype),
        ),
        grid_spec=pltpu.PrefetchScalarGridSpec(
            num_scalar_prefetch=1,
            grid=(rows // each,),
            in_specs=[
                pl.BlockSpec((each, depth, orbitals), lambda i, m: (i, 0, 0)),
                pl.BlockSpec((each, orbitals, columns), lambda i, m: (i, 0, 0)),
                edge,
            ],
            out_specs=[edge, pl.BlockSpec((rows * share, columns), lambda i, m: (0, 0)), edge, edge],
            scratch_shapes=[
                pltpu.VMEM((sets, (slots + group - 1) * share, group * orbitals), jnp.bfloat16),
                pltpu.VMEM(((rows + 2 * reach) * share, columns), jnp.float32),
            ],
        ),
        compiler_params=pltpu.CompilerParams(
            dimension_semantics=(ARBITRARY,), vmem_limit_bytes=VMEM_BYTES
        ),
        cost_estimate=pl.CostEstimate(flops=flops, bytes_accessed=ham.size * 2, transcendentals=0),
        name="push_blocks",
    )(mask, ham, cotangent, term)


def pull_kernel(
    first_row, each, carried, slots, share, mask_ref, side_ref, ham_ref, slope_ref, cot_ref, prev_ref, head_ref, tail_ref, *rest,
):
    keep_ref, send_ref, force_ref = rest[carried : carried + 3]
    window, both, product = rest[-3:]
    step = pl.program_id(0)
    orbitals = ham_ref.shape[2]
    side = side_ref[0]

    @pl.when(step == 0)
    def _():
        split = head_ref.shape[0]
        window[:split, :] = head_ref[...]
        window[split:, :] = tail_ref[...]

    mine = pl.multiple_of(side * share, share)
    other = pl.multiple_of((1 - side) * share, share)
    for k in range(each):
        at = step * each + k
        row = first_row + at
        for slot in range(slots):
            kept = mask_ref[row, slot] != 0
            span = slice(slot * share, (slot + 1) * share)
            block = ham_ref[k, span, :]
            both[k, span, :orbitals] = jnp.where(kept, block, jnp.zeros_like(block))
            block = slope_ref[k, span, :]
            both[k, span, orbitals:] = jnp.where(kept, block, jnp.zeros_like(block))
        near = window[pl.ds(pl.multiple_of(at * share, share), slots * share), :]
        product[k] = lax.dot_general(
            both[k], near, (((0,), (0,)), ((), ())), preferred_element_type=jnp.float32
        )
        keep_ref[k] = 2.0 * product[k, pl.ds(mine, share), :] - prev_ref[k].astype(jnp.float32)
        send_ref[k] = (2.0 * product[k, pl.ds(other, share), :]).astype(send_ref.dtype)
        work = product[k, orbitals:, :] * cot_ref[k].astype(jnp.float32)
        lanes = 128
        folded = work[:, :lanes]
        for lane in range(lanes, work.shape[1], lanes):
            folded = folded + work[:, lane : lane + lanes]
        force_ref[k] = 2.0 * jnp.sum(folded.T, axis=0, keepdims=True)


def pull(ham, slope, mask, side, cotangent, previous, head, tail, share, first_row, rows, carried, keep):
    total_rows, depth, orbitals = ham.shape
    columns = cotangent.shape[2]
    slots = depth // share
    each = largest_divisor(rows, 3)
    skip = first_row // each
    assert skip * each == first_row
    held = tuple(carried) + ((keep,) if keep is not None else ())
    kernel = functools.partial(pull_kernel, first_row, each, len(held) + len(carried), slots, share)
    flops = 4 * rows * depth * orbitals * columns
    row_block = lambda *dims: pl.BlockSpec((each,) + dims, lambda i, m, s: (i + skip, 0, 0))
    whole = lambda a: pl.BlockSpec(a.shape, lambda i, m, s: (0, 0))
    out_block = lambda *dims: pl.BlockSpec((each,) + dims, lambda i, m, s: (i, 0, 0))
    anywhere = pl.BlockSpec(memory_space=pl.ANY)
    inputs = (mask, side, ham, slope, cotangent, previous, head, tail)
    aliases = {len(inputs) + k: k for k in range(len(held))}
    return pl.pallas_call(
        kernel,
        out_shape=tuple(jax.ShapeDtypeStruct(a.shape, a.dtype) for a in carried)
        + (
            jax.ShapeDtypeStruct((total_rows, share, columns), jnp.float32),
            jax.ShapeDtypeStruct((rows, share, columns), jnp.bfloat16),
            jax.ShapeDtypeStruct((rows, 1, orbitals), jnp.float32),
        ),
        grid_spec=pltpu.PrefetchScalarGridSpec(
            num_scalar_prefetch=2,
            grid=(rows // each,),
            in_specs=[
                row_block(depth, orbitals),
                row_block(depth, orbitals),
                row_block(orbitals, columns),
                row_block(share, columns),
                whole(head),
                whole(tail),
            ]
            + [anywhere] * len(held),
            out_specs=[anywhere] * len(carried)
            + [
                row_block(share, columns),
                out_block(share, columns),
                out_block(1, orbitals),
            ],
            scratch_shapes=[
                pltpu.VMEM((head.shape[0] + tail.shape[0], columns), jnp.bfloat16),
                pltpu.VMEM((each, depth, 2 * orbitals), jnp.bfloat16),
                pltpu.VMEM((each, 2 * orbitals, columns), jnp.float32),
            ],
        ),
        input_output_aliases=aliases,
        compiler_params=pltpu.CompilerParams(
            dimension_semantics=(ARBITRARY,), vmem_limit_bytes=PULL_VMEM_BYTES
        ),
        cost_estimate=pl.CostEstimate(
            flops=flops, bytes_accessed=4 * rows * depth * orbitals, transcendentals=0
        ),
        name="pull_blocks",
    )(*inputs, *held)


def add_kernel(steps, own_ref, first_ref, second_ref, *rest):
    out_ref = rest[-1]
    step = pl.program_id(0)

    @pl.when(step < steps)
    def _():
        out_ref[...] = (own_ref[...] + first_ref[...].astype(jnp.float32)).astype(out_ref.dtype)

    @pl.when(step >= steps)
    def _():
        out_ref[...] = (own_ref[...] + second_ref[...].astype(jnp.float32)).astype(out_ref.dtype)


def add_parts(own, arrived, size, places, filled):
    columns = own.shape[1]
    steps = 1
    piece = size // steps
    (one, one_at), (two, two_at) = arrived

    def spec(first_at, second_at, turn):
        def place(i):
            near = jnp.minimum(i, steps - 1) if turn == 0 else i
            far = jnp.maximum(i - steps, 0)
            if turn == 0:
                return (first_at * steps + near, 0)
            if turn == 1:
                return (second_at * steps + far, 0)
            return (jnp.where(i < steps, first_at * steps + i, second_at * steps + i - steps), 0)

        return pl.BlockSpec((piece, columns), place)

    held = () if filled is None else (filled,)
    return pl.pallas_call(
        functools.partial(add_kernel, steps),
        out_shape=jax.ShapeDtypeStruct(own.shape, jnp.bfloat16),
        grid=(2 * steps,),
        in_specs=[spec(*places, 2), spec(one_at, 0, 0), spec(0, two_at, 1)]
        + [pl.BlockSpec(memory_space=pl.ANY)] * len(held),
        out_specs=spec(*places, 2),
        input_output_aliases={3: 0} if held else {},
        compiler_params=pltpu.CompilerParams(
            dimension_semantics=(ARBITRARY,), vmem_limit_bytes=8 * 1024 * 1024
        ),
        cost_estimate=pl.CostEstimate(flops=0, bytes_accessed=0, transcendentals=0),
        name="add_parts",
    )(own, one, two, *held)


def local(term_now, term_prev, cotangent, ham_blocks, block_mask, ham_slope, atom_owner):
    rows, slots, share, orbitals = ham_blocks.shape
    columns = term_now.shape[2]
    reach = (slots - 1) // 2
    edge = reach * share
    half = rows // 2
    ham = ham_blocks.reshape(rows, slots * share, orbitals)
    slope = ham_slope.reshape(rows, slots * share, orbitals)
    term = term_now.reshape(rows * share, columns)
    side = lax.axis_index("layers").astype(jnp.int32).reshape(1)

    below = shifted(term[rows * share - edge :], "rows", 1)
    to_below, own, to_above, first_edge = push(ham, block_mask, cotangent, term, share)
    above = shifted(first_edge, "rows", -1)

    args = (ham, slope, block_mask, side, cotangent, term_prev)
    to_above, keep, send_a, force_a = pull(*args, below, term, share, 0, half, (to_above,), None)
    from_below = shifted(to_above, "rows", 1)
    got_a = swapped(send_a, "layers", 1)
    paired = 2 if lax.axis_size("cols") % 2 == 0 else 1
    other_a = swapped(force_a, "cols", 1) if paired == 2 else jnp.zeros_like(force_a)
    other_a, to_below, keep, send_b, force_b = pull(
        *args, term, above, share, half, rows - half, (other_a, to_below), keep
    )
    force_a = force_a + other_a
    got_b = swapped(send_b, "layers", 1)
    from_above = shifted(to_below, "rows", -1)

    row_force = jnp.concatenate([force_a, force_b], axis=0).reshape(rows, orbitals)
    atom_ids = lax.broadcasted_iota(jnp.int32, (1, 1, APB), 2)
    owned = jnp.where(atom_owner[:, :, None] == atom_ids, row_force[:, :, None], 0.0)
    forces = jnp.sum(owned, axis=1)
    gathered = lax.all_gather(forces, "cols")
    forces = jnp.concatenate(
        [jnp.sum(gathered[::paired, :half], axis=0), jnp.sum(gathered[:, half:], axis=0)], axis=0
    )
    others = swapped(forces, "layers", 1)

    keep = keep.reshape(rows * share, columns)
    got_a = got_a.reshape(half * share, columns)
    got_b = got_b.reshape((rows - half) * share, columns)
    size = edge // 2
    term_next = add_parts(keep, ((got_a, 0), (got_a, 1)), size, (0, 1), None)
    from_below, term_next = lax.optimization_barrier((from_below, term_next))
    grad_term = add_parts(own, ((from_below, 0), (from_below, 1)), size, (0, 1), None)
    got_b, grad_term = lax.optimization_barrier((got_b, grad_term))
    term_next = add_parts(keep, ((got_b, 0), (got_b, 1)), size, (2, 3), term_next)
    others, term_next = lax.optimization_barrier((others, term_next))
    forces = forces + others
    from_above, term_next, forces = lax.optimization_barrier((from_above, term_next, forces))
    grad_term = add_parts(own, ((from_above, 0), (from_above, 1)), size, (2, 3), grad_term)
    shape = (rows, share, columns)
    return (term_next.reshape(shape), grad_term.reshape(shape), forces)


def solution(mesh):
    return jax.shard_map(
        local,
        mesh=mesh,
        in_specs=(
            P("rows", "layers", "cols"),
            P("rows", "layers", "cols"),
            P("rows", None, "cols"),
            P("rows", None, "layers", None),
            P("rows", None),
            P("rows", None, "layers", None),
            P("rows", None),
        ),
        out_specs=(P("rows", "layers", "cols"), P("rows", "layers", "cols"), P("rows", None)),
        check_vma=False,
    )
```

```python
import functools

import jax
import jax.numpy as jnp
from jax import lax
from jax.experimental import pallas as pl
from jax.experimental.pallas import tpu as pltpu
from jax.sharding import PartitionSpec as P

APB = 64
VMEM_BYTES = 62 * 1024 * 1024
PULL_VMEM_BYTES = 51 * 1024 * 1024
ARBITRARY = pltpu.GridDimensionSemantics.ARBITRARY


def shifted(value, axis, steps):
    count = lax.axis_size(axis)
    pairs = [(source, (source + steps) % count) for source in range(count)]
    return lax.ppermute(value, axis, pairs)


def swapped(value, axis, bit):
    count = lax.axis_size(axis)
    return lax.ppermute(value, axis, [(source, source ^ bit) for source in range(count)])


def push_kernel(
    group, sets, slots, share, mask_ref, ham_ref, cot_ref, edge_ref, low_ref, own_ref, high_ref, copy_ref, left, total
):
    step = pl.program_id(0)
    orbitals = ham_ref.shape[2]
    columns = cot_ref.shape[2]
    spread = (slots + group - 1) * share

    @pl.when(step == 0)
    def _():
        total[...] = jnp.zeros_like(total)
        left[...] = jnp.zeros_like(left)
        copy_ref[...] = edge_ref[...]

    for part in range(sets):
        base = part * group
        for k in range(group):
            row = step * (sets * group) + base + k
            for slot in range(slots):
                kept = mask_ref[row, slot] != 0
                block = ham_ref[base + k, slot * share : (slot + 1) * share, :]
                at = (slot + k) * share
                left[part, at : at + share, k * orbitals : (k + 1) * orbitals] = jnp.where(
                    kept, block, jnp.zeros_like(block)
                )
        right = cot_ref[base : base + group].reshape(group * orbitals, columns)
        first = pl.multiple_of((step * sets + part) * (group * share), group * share)
        piece = 2 * share
        for at in range(0, spread, piece):
            size = min(piece, spread - at)
            total[pl.ds(first + at, size), :] += jnp.dot(
                left[part, at : at + size, :], right, preferred_element_type=jnp.float32
            )

    @pl.when(step == pl.num_programs(0) - 1)
    def _():
        halo = low_ref.shape[0]
        own = own_ref.shape[0]
        low_ref[...] = (2.0 * total[:halo, :]).astype(low_ref.dtype)
        own_ref[...] = 2.0 * total[halo : halo + own, :]
        high_ref[...] = (2.0 * total[halo + own :, :]).astype(high_ref.dtype)


def largest_divisor(count, limit):
    return max(k for k in range(1, limit + 1) if count % k == 0)


def push(ham, mask, cotangent, term, share):
    rows, depth, orbitals = ham.shape
    columns = cotangent.shape[2]
    slots = depth // share
    reach = (slots - 1) // 2
    group = largest_divisor(rows, 6)
    sets = largest_divisor(rows // group, 2)
    each = group * sets
    kernel = functools.partial(push_kernel, group, sets, slots, share)
    flops = 2 * rows * depth * orbitals * columns
    edge = pl.BlockSpec((reach * share, columns), lambda i, m: (0, 0))
    return pl.pallas_call(
        kernel,
        out_shape=(
            jax.ShapeDtypeStruct((reach * share, columns), jnp.bfloat16),
            jax.ShapeDtypeStruct((rows * share, columns), jnp.float32),
            jax.ShapeDtypeStruct((reach * share, columns), jnp.bfloat16),
            jax.ShapeDtypeStruct((reach * share, columns), term.dtype),
        ),
        grid_spec=pltpu.PrefetchScalarGridSpec(
            num_scalar_prefetch=1,
            grid=(rows // each,),
            in_specs=[
                pl.BlockSpec((each, depth, orbitals), lambda i, m: (i, 0, 0)),
                pl.BlockSpec((each, orbitals, columns), lambda i, m: (i, 0, 0)),
                edge,
            ],
            out_specs=[edge, pl.BlockSpec((rows * share, columns), lambda i, m: (0, 0)), edge, edge],
            scratch_shapes=[
                pltpu.VMEM((sets, (slots + group - 1) * share, group * orbitals), jnp.bfloat16),
                pltpu.VMEM(((rows + 2 * reach) * share, columns), jnp.float32),
            ],
        ),
        compiler_params=pltpu.CompilerParams(
            dimension_semantics=(ARBITRARY,), vmem_limit_bytes=VMEM_BYTES
        ),
        cost_estimate=pl.CostEstimate(flops=flops, bytes_accessed=ham.size * 2, transcendentals=0),
        name="push_blocks",
    )(mask, ham, cotangent, term)


def pull_kernel(
    first_row, each, carried, slots, share, mask_ref, side_ref, ham_ref, slope_ref, cot_ref, prev_ref, head_ref, tail_ref, *rest,
):
    keep_ref, send_ref, force_ref = rest[carried : carried + 3]
    window, both, product = rest[-3:]
    step = pl.program_id(0)
    orbitals = ham_ref.shape[2]
    side = side_ref[0]

    @pl.when(step == 0)
    def _():
        split = head_ref.shape[0]
        window[:split, :] = head_ref[...]
        window[split:, :] = tail_ref[...]

    mine = pl.multiple_of(side * share, share)
    other = pl.multiple_of((1 - side) * share, share)
    for k in range(each):
        at = step * each + k
        row = first_row + at
        for slot in range(slots):
            kept = mask_ref[row, slot] != 0
            span = slice(slot * share, (slot + 1) * share)
            block = ham_ref[k, span, :]
            both[k, span, :orbitals] = jnp.where(kept, block, jnp.zeros_like(block))
            block = slope_ref[k, span, :]
            both[k, span, orbitals:] = jnp.where(kept, block, jnp.zeros_like(block))
    for k in range(each):
        at = step * each + k
        near = window[pl.ds(pl.multiple_of(at * share, share), slots * share), :]
        product[k] = lax.dot_general(
            both[k], near, (((0,), (0,)), ((), ())), preferred_element_type=jnp.float32
        )
    for k in range(each):
        keep_ref[k] = 2.0 * product[k, pl.ds(mine, share), :] - prev_ref[k].astype(jnp.float32)
        send_ref[k] = (2.0 * product[k, pl.ds(other, share), :]).astype(send_ref.dtype)
        work = product[k, orbitals:, :] * cot_ref[k].astype(jnp.float32)
        lanes = 128
        folded = work[:, :lanes]
        for lane in range(lanes, work.shape[1], lanes):
            folded = folded + work[:, lane : lane + lanes]
        force_ref[k] = 2.0 * jnp.sum(folded.T, axis=0, keepdims=True)


def pull(ham, slope, mask, side, cotangent, previous, head, tail, share, first_row, rows, carried, keep):
    total_rows, depth, orbitals = ham.shape
    columns = cotangent.shape[2]
    slots = depth // share
    each = largest_divisor(rows, 3)
    skip = first_row // each
    assert skip * each == first_row
    held = tuple(carried) + ((keep,) if keep is not None else ())
    kernel = functools.partial(pull_kernel, first_row, each, len(held) + len(carried), slots, share)
    flops = 4 * rows * depth * orbitals * columns
    row_block = lambda *dims: pl.BlockSpec((each,) + dims, lambda i, m, s: (i + skip, 0, 0))
    whole = lambda a: pl.BlockSpec(a.shape, lambda i, m, s: (0, 0))
    out_block = lambda *dims: pl.BlockSpec((each,) + dims, lambda i, m, s: (i, 0, 0))
    anywhere = pl.BlockSpec(memory_space=pl.ANY)
    inputs = (mask, side, ham, slope, cotangent, previous, head, tail)
    aliases = {len(inputs) + k: k for k in range(len(held))}
    return pl.pallas_call(
        kernel,
        out_shape=tuple(jax.ShapeDtypeStruct(a.shape, a.dtype) for a in carried)
        + (
            jax.ShapeDtypeStruct((total_rows, share, columns), jnp.float32),
            jax.ShapeDtypeStruct((rows, share, columns), jnp.bfloat16),
            jax.ShapeDtypeStruct((rows, 1, orbitals), jnp.float32),
        ),
        grid_spec=pltpu.PrefetchScalarGridSpec(
            num_scalar_prefetch=2,
            grid=(rows // each,),
            in_specs=[
                row_block(depth, orbitals),
                row_block(depth, orbitals),
                row_block(orbitals, columns),
                row_block(share, columns),
                whole(head),
                whole(tail),
            ]
            + [anywhere] * len(held),
            out_specs=[anywhere] * len(carried)
            + [
                row_block(share, columns),
                out_block(share, columns),
                out_block(1, orbitals),
            ],
            scratch_shapes=[
                pltpu.VMEM((head.shape[0] + tail.shape[0], columns), jnp.bfloat16),
                pltpu.VMEM((each, depth, 2 * orbitals), jnp.bfloat16),
                pltpu.VMEM((each, 2 * orbitals, columns), jnp.float32),
            ],
        ),
        input_output_aliases=aliases,
        compiler_params=pltpu.CompilerParams(
            dimension_semantics=(ARBITRARY,), vmem_limit_bytes=PULL_VMEM_BYTES
        ),
        cost_estimate=pl.CostEstimate(
            flops=flops, bytes_accessed=4 * rows * depth * orbitals, transcendentals=0
        ),
        name="pull_blocks",
    )(*inputs, *held)


def add_kernel(steps, own_ref, first_ref, second_ref, *rest):
    out_ref = rest[-1]
    step = pl.program_id(0)

    @pl.when(step < steps)
    def _():
        out_ref[...] = (own_ref[...] + first_ref[...].astype(jnp.float32)).astype(out_ref.dtype)

    @pl.when(step >= steps)
    def _():
        out_ref[...] = (own_ref[...] + second_ref[...].astype(jnp.float32)).astype(out_ref.dtype)


def add_parts(own, arrived, size, places, filled):
    columns = own.shape[1]
    steps = 1
    piece = size // steps
    (one, one_at), (two, two_at) = arrived

    def spec(first_at, second_at, turn):
        def place(i):
            near = jnp.minimum(i, steps - 1) if turn == 0 else i
            far = jnp.maximum(i - steps, 0)
            if turn == 0:
                return (first_at * steps + near, 0)
            if turn == 1:
                return (second_at * steps + far, 0)
            return (jnp.where(i < steps, first_at * steps + i, second_at * steps + i - steps), 0)

        return pl.BlockSpec((piece, columns), place)

    held = () if filled is None else (filled,)
    return pl.pallas_call(
        functools.partial(add_kernel, steps),
        out_shape=jax.ShapeDtypeStruct(own.shape, jnp.bfloat16),
        grid=(2 * steps,),
        in_specs=[spec(*places, 2), spec(one_at, 0, 0), spec(0, two_at, 1)]
        + [pl.BlockSpec(memory_space=pl.ANY)] * len(held),
        out_specs=spec(*places, 2),
        input_output_aliases={3: 0} if held else {},
        compiler_params=pltpu.CompilerParams(
            dimension_semantics=(ARBITRARY,), vmem_limit_bytes=8 * 1024 * 1024
        ),
        cost_estimate=pl.CostEstimate(flops=0, bytes_accessed=0, transcendentals=0),
        name="add_parts",
    )(own, one, two, *held)


def local(term_now, term_prev, cotangent, ham_blocks, block_mask, ham_slope, atom_owner):
    rows, slots, share, orbitals = ham_blocks.shape
    columns = term_now.shape[2]
    reach = (slots - 1) // 2
    edge = reach * share
    half = rows // 2
    ham = ham_blocks.reshape(rows, slots * share, orbitals)
    slope = ham_slope.reshape(rows, slots * share, orbitals)
    term = term_now.reshape(rows * share, columns)
    side = lax.axis_index("layers").astype(jnp.int32).reshape(1)

    below = shifted(term[rows * share - edge :], "rows", 1)
    to_below, own, to_above, first_edge = push(ham, block_mask, cotangent, term, share)
    above = shifted(first_edge, "rows", -1)

    args = (ham, slope, block_mask, side, cotangent, term_prev)
    to_above, keep, send_a, force_a = pull(*args, below, term, share, 0, half, (to_above,), None)
    from_below = shifted(to_above, "rows", 1)
    got_a = swapped(send_a, "layers", 1)
    paired = 2 if lax.axis_size("cols") % 2 == 0 else 1
    other_a = swapped(force_a, "cols", 1) if paired == 2 else jnp.zeros_like(force_a)
    other_a, to_below, keep, send_b, force_b = pull(
        *args, term, above, share, half, rows - half, (other_a, to_below), keep
    )
    force_a = force_a + other_a
    got_b = swapped(send_b, "layers", 1)
    from_above = shifted(to_below, "rows", -1)

    row_force = jnp.concatenate([force_a, force_b], axis=0).reshape(rows, orbitals)
    atom_ids = lax.broadcasted_iota(jnp.int32, (1, 1, APB), 2)
    owned = jnp.where(atom_owner[:, :, None] == atom_ids, row_force[:, :, None], 0.0)
    forces = jnp.sum(owned, axis=1)
    gathered = lax.all_gather(forces, "cols")
    forces = jnp.concatenate(
        [jnp.sum(gathered[::paired, :half], axis=0), jnp.sum(gathered[:, half:], axis=0)], axis=0
    )
    others = swapped(forces, "layers", 1)

    keep = keep.reshape(rows * share, columns)
    got_a = got_a.reshape(half * share, columns)
    got_b = got_b.reshape((rows - half) * share, columns)
    size = edge // 2
    term_next = add_parts(keep, ((got_a, 0), (got_a, 1)), size, (0, 1), None)
    from_below, term_next = lax.optimization_barrier((from_below, term_next))
    grad_term = add_parts(own, ((from_below, 0), (from_below, 1)), size, (0, 1), None)
    got_b, grad_term = lax.optimization_barrier((got_b, grad_term))
    term_next = add_parts(keep, ((got_b, 0), (got_b, 1)), size, (2, 3), term_next)
    others, term_next = lax.optimization_barrier((others, term_next))
    forces = forces + others
    from_above, term_next, forces = lax.optimization_barrier((from_above, term_next, forces))
    grad_term = add_parts(own, ((from_above, 0), (from_above, 1)), size, (2, 3), grad_term)
    shape = (rows, share, columns)
    return (term_next.reshape(shape), grad_term.reshape(shape), forces)


def solution(mesh):
    return jax.shard_map(
        local,
        mesh=mesh,
        in_specs=(
            P("rows", "layers", "cols"),
            P("rows", "layers", "cols"),
            P("rows", None, "cols"),
            P("rows", None, "layers", None),
            P("rows", None),
            P("rows", None, "layers", None),
            P("rows", None),
        ),
        out_specs=(P("rows", "layers", "cols"), P("rows", "layers", "cols"), P("rows", None)),
        check_vma=False,
    )
```
